32 devices in a mesh: ctx: 8 (over y, x, core), head: 4 (over z).
Axes of the slice: x: 2, y: 2, z: 4, core: 2. Of those that a mesh axis runs over, the one named last changes fastest.
Arguments:
- queries: bfloat16 [2048, 2048], P('ctx', 'head'), may hold values from -6 to 6
- keys: bfloat16 [2048, 2, 2048], P('ctx', None, 'head'), may hold values from -6 to 6
- values: bfloat16 [2048, 2, 2048], P('ctx', None, 'head'), may hold values from -6 to 6
- beta: float32 [16, 2, 2048], P('head', None, 'ctx'), as said below
- log_gate: float32 [16, 2048], P('head', 'ctx'), as said below
- norm_gain: float32 [2048], P('head'), may hold values from 0.1 to 1.9
- out_weight: bfloat16 [2048, 4096], P('head'), may hold values from -0.125 to 0.125
Outputs:
- mixed: bfloat16 [2048, 4096], P(('ctx', 'head'))
The draws below stay inside these ranges and needn't reach their ends.
Inputs may be any that keep to these rules, and one draw needn't show every extreme that they name: `beta`: strictly below 2. `log_gate`: never positive.
All inputs are finite; a program needn't handle non-finite values.
Results may differ from the reference program's by a relative error of at most 0.025.
Values may be sent and summed in bfloat16 or wider, within the bound.
A program may use at most 128 MiB of HBM per device.

```python
import jax
import jax.numpy as jnp
from jax import lax

D = 4096
DH = 128
HEAD_DEV = 4
CT = 32
HEAD_TOTAL = 16
TOKEN_TOTAL = 2048
N_HEAD = 4


def slow_heads(key):
    chosen = jax.random.uniform(jax.random.fold_in(key, 11), (HEAD_TOTAL,), jnp.float32)
    slow_share = 0.5
    return chosen < slow_share


def rough_factor(key, shape):
    return jnp.exp(jax.random.uniform(key, shape, jnp.float32, jnp.log(0.5), jnp.log(2.0)))


def draw_beta(key, part):
    slow_mask = slow_heads(key)[:, None, None]
    first_key, second_key, extra_random_key = jax.random.split(jax.random.fold_in(key, 21), 3)
    margin = jnp.exp(jax.random.uniform(first_key, (HEAD_TOTAL, 1, 1), jnp.float32, jnp.log(0.03), jnp.log(0.25))) * DH / (2.0 * TOKEN_TOTAL)
    slow_beta = 2.0 - margin * rough_factor(second_key, (HEAD_TOTAL, 2, TOKEN_TOTAL))
    fast_beta = jax.random.uniform(extra_random_key, (HEAD_TOTAL, 2, TOKEN_TOTAL), jnp.float32, 0.1, 1.9)
    return jnp.where(slow_mask, slow_beta, fast_beta)


def draw_log_gate(key, part):
    slow_mask = slow_heads(key)[:, None]
    first_key, second_key, extra_random_key, fourth_key = jax.random.split(jax.random.fold_in(key, 31), 4)
    fast_rate = jnp.exp(jax.random.uniform(first_key, (HEAD_TOTAL, 1), jnp.float32, jnp.log(1.0 / 50.0), jnp.log(1.0 / 15.0)))
    head_rate = jnp.where(slow_mask, 0.2 / TOKEN_TOTAL, fast_rate)
    baseline_log_gates = -head_rate * rough_factor(second_key, (HEAD_TOTAL, TOKEN_TOTAL))
    token_span_width = jax.random.uniform(extra_random_key, (HEAD_TOTAL, TOKEN_TOTAL), jnp.float32) < 2.0 / TOKEN_TOTAL
    decay_log_terms = jnp.log(jax.random.uniform(fourth_key, (HEAD_TOTAL, TOKEN_TOTAL), jnp.float32, 0.5, 0.8))
    return baseline_log_gates + jnp.where(token_span_width, decay_log_terms, 0.0)


def shard_levels(key, shape, cuts, low, largest):
    loudness, own = 1.0, jax.random.fold_in(key, 6)
    for axis_at, blocks in cuts:
        steps = jnp.exp(jax.random.uniform(jax.random.fold_in(own, axis_at), (blocks,), jnp.float32, low / len(cuts), largest / len(cuts)))
        loudness = loudness * jnp.repeat(steps, shape[axis_at] // blocks).reshape([-1 if axis == axis_at else 1 for axis in range(len(shape))])
    return loudness


def centred(stream_key, dims, deviation, reach, cuts=(), kind=jnp.bfloat16):
    result = jax.random.normal(stream_key, dims, jnp.float32) * deviation
    if len(cuts) > 0:
        result = shard_levels(stream_key, dims, cuts, -0.22, 0.18) * result
    return jnp.clip(result, min=-reach, max=reach).astype(kind)


def setup_inputs(seed: int = 0) -> dict:
    key_list = jax.random.split(jax.random.key(seed), 8)
    queries = centred(key_list[0], (TOKEN_TOTAL, HEAD_TOTAL * DH), 1.0, 6.0, ((0, 8), (1, 4)))
    keys = centred(key_list[1], (TOKEN_TOTAL, 2, HEAD_TOTAL * DH), 1.0, 6.0, ((0, 8), (2, 4)))
    values = centred(key_list[2], (TOKEN_TOTAL, 2, HEAD_TOTAL * DH), 1.0, 6.0, ((0, 8), (2, 4)))
    beta = draw_beta(jax.random.fold_in(key_list[7], 71), 0)
    log_gate = draw_log_gate(jax.random.fold_in(key_list[7], 71), 0)
    norm_gain = jnp.clip(1.0 + 0.18 * jax.random.normal(key_list[5], (HEAD_TOTAL * DH,), jnp.float32), 0.1, 1.9)
    out_weight = centred(key_list[6], (HEAD_TOTAL * DH, D), (HEAD_TOTAL * DH) ** -0.5, 0.125, ((0, 4),))
    return dict(queries=queries, keys=keys, values=values, beta=beta, log_gate=log_gate, norm_gain=norm_gain, out_weight=out_weight)


highest = lax.Precision.HIGHEST

def normalize(key_rows):
    return key_rows * lax.rsqrt(lax.optimization_barrier(jnp.sum(key_rows * key_rows, axis=-1, keepdims=True)) + 1e-06)

def span_terms(query_rows, key_rows, value_rows, beta_values_rows, gate_rows):
    step_count = key_rows.shape[-2]
    cumulative = jnp.cumsum(gate_rows, axis=-1)
    later_step = jnp.arange(step_count)[:, None]
    earlier_step = jnp.arange(step_count)[None, :]
    strict = later_step > earlier_step
    gap_logs = cumulative[..., :, None] - cumulative[..., None, :]
    decay_ratio = jnp.where(strict, jnp.exp(jnp.where(strict, gap_logs, 0.0)), 0.0)
    key_inner = jnp.einsum('...sd,...rd->...sr', key_rows, key_rows, precision=highest)
    lower_part = decay_ratio * beta_values_rows[..., None, :] * key_inner
    system = jnp.eye(step_count, dtype=key_rows.dtype) + lower_part
    right_side = jnp.concatenate([value_rows, jnp.exp(cumulative)[..., None] * key_rows], axis=-1)
    solved = lax.linalg.triangular_solve(system, right_side, left_side=True, lower=True, unit_diagonal=True)
    value_width = value_rows.shape[-1]
    fresh_values = solved[..., :value_width]
    carried = solved[..., value_width:]
    span_total = cumulative[..., -1]
    scaled = (jnp.exp(span_total[..., None] - cumulative) * beta_values_rows)[..., None] * key_rows
    identity_key = jnp.eye(key_rows.shape[-1], dtype=key_rows.dtype)
    transition = jnp.exp(span_total)[..., None, None] * identity_key - jnp.einsum('...rd,...re->...de', scaled, carried, precision=highest)
    offset = jnp.einsum('...rd,...re->...de', scaled, fresh_values, precision=highest)
    read_logs = cumulative[..., 1::2]
    row_index = jnp.arange(query_rows.shape[-2])[:, None]
    visible = 2 * row_index + 1 >= earlier_step
    read_gaps = read_logs[..., :, None] - cumulative[..., None, :]
    weight = jnp.where(visible, jnp.exp(jnp.where(visible, read_gaps, 0.0)), 0.0)
    scores = jnp.einsum('...td,...rd->...tr', query_rows, key_rows, precision=highest) * weight * beta_values_rows[..., None, :]
    lead_rows = jnp.exp(read_logs)[..., None] * query_rows - jnp.einsum('...tr,...re->...te', scores, carried, precision=highest)
    local_part = jnp.einsum('...tr,...re->...te', scores, fresh_values, precision=highest)
    return (transition, offset, lead_rows, local_part)

def reference(queries, keys, values, beta, log_gate, norm_gain, out_weight):
    spans = TOKEN_TOTAL // CT
    query_all = queries.reshape(spans, CT, HEAD_TOTAL, DH)
    key_all = keys.reshape(spans, CT, 2, HEAD_TOTAL, DH).reshape(spans, 2 * CT, HEAD_TOTAL, DH)
    value_all = values.reshape(spans, CT, 2, HEAD_TOTAL, DH).reshape(spans, 2 * CT, HEAD_TOTAL, DH)
    beta_all = jnp.transpose(beta, (2, 1, 0)).reshape(spans, 2 * CT, HEAD_TOTAL)
    gate_pair = jnp.stack([log_gate.T, jnp.zeros_like(log_gate.T)], axis=1)
    gate_all = gate_pair.reshape(spans, 2 * CT, HEAD_TOTAL)
    head_gain = norm_gain.reshape(HEAD_TOTAL, 1, DH)

    def advance(memory, inputs):
        query_block, key_block, value_block, beta_block, gate_block = inputs
        query_rows = jnp.swapaxes(query_block.astype(jnp.float32), 0, 1)
        key_rows = normalize(jnp.swapaxes(key_block.astype(jnp.float32), 0, 1))
        value_rows = jnp.swapaxes(value_block.astype(jnp.float32), 0, 1)
        transition, offset, lead_rows, local_part = span_terms(query_rows, key_rows, value_rows, beta_block.T, gate_block.T)
        read_rows = jnp.einsum('htd,hde->hte', lead_rows, memory, precision=highest) + local_part
        row_scale = lax.rsqrt(lax.optimization_barrier(jnp.mean(read_rows * read_rows, axis=-1, keepdims=True)) + 1e-06)
        normed = read_rows * row_scale * head_gain
        out_rows = jnp.swapaxes(normed, 0, 1).reshape(CT, HEAD_TOTAL * DH).astype(jnp.bfloat16)
        updated = jnp.einsum('hde,hef->hdf', transition, memory, precision=highest) + offset
        return (updated, out_rows)
    start_memory = jnp.zeros((HEAD_TOTAL, DH, DH), jnp.float32)
    _, blocks = lax.scan(advance, start_memory, (query_all, key_all, value_all, beta_all, gate_all))
    flat_rows = blocks.reshape(TOKEN_TOTAL, HEAD_TOTAL * DH)
    group_width = HEAD_DEV * DH
    summed = jnp.zeros((TOKEN_TOTAL, D), jnp.float32)
    for group_index in range(N_HEAD):
        low = group_index * group_width
        partial_value = jnp.dot(flat_rows[:, low:low + group_width].astype(jnp.float32), out_weight[low:low + group_width].astype(jnp.float32), preferred_element_type=jnp.float32).astype(jnp.bfloat16)
        summed = summed + partial_value.astype(jnp.float32)
    return summed.astype(jnp.bfloat16)
```

```python
import functools

import jax
import jax.numpy as jnp
from jax import lax
from jax.experimental import pallas as pl
from jax.experimental.pallas import tpu as pltpu
from jax.sharding import PartitionSpec as P

DH = 128
F32 = jnp.float32
BF16 = jnp.bfloat16
highest = lax.Precision.HIGHEST


def mm(a, b):
    return jnp.dot(a, b, preferred_element_type=F32)


def halves(x):
    high = x.astype(BF16)
    return high, (x - high.astype(F32)).astype(BF16)


def mm_split(a, b):
    a_high, a_low = halves(a)
    b_high, b_low = halves(b)
    left = jnp.concatenate([a_high, a_low], axis=1)
    row = jnp.concatenate([b_high, b_low], axis=1)
    wide = mm(left, jnp.concatenate([row, row], axis=0))
    n = b.shape[1]
    return wide[:, :n] + wide[:, n:]


def iota(shape, axis):
    return lax.broadcasted_iota(jnp.int32, shape, axis)


def local_kernel(heads, tokens, q_ref, k_ref, v_ref, beta_ref, gate_ref, lead_ref, loc_ref, m_ref, o_ref):
    span = 64 if tokens % 64 == 0 else tokens
    steps = 2 * span
    chunks = tokens // span
    gate = jnp.maximum(gate_ref[...], -1000.0)
    t_at, s_at = iota((tokens, 2 * tokens), 0), iota((tokens, 2 * tokens), 1)
    same = (t_at // span) == (s_at // steps)
    until = (same & (2 * t_at <= s_at)).astype(F32)
    exact = functools.partial(jnp.dot, precision=highest, preferred_element_type=F32)
    cum = exact(gate, until)
    beta = exact(beta_ref[:, 0, :], (2 * t_at == s_at).astype(F32)) + exact(
        beta_ref[:, 1, :], (2 * t_at + 1 == s_at).astype(F32)
    )
    r_at, c_at = iota((tokens, tokens), 0), iota((tokens, tokens), 1)
    read = exact(gate, (((r_at // span) == (c_at // span)) & (r_at <= c_at)).astype(F32))
    pad = jnp.zeros((8 - heads % 8, 2 * tokens), F32) if heads % 8 else None
    if pad is not None:
        cum_columns = jnp.concatenate([cum, pad], axis=0).T
        read_columns = jnp.concatenate([read, pad[:, :tokens]], axis=0).T
        beta_columns = jnp.concatenate([beta, pad], axis=0).T
    else:
        cum_columns, read_columns, beta_columns = cum.T, read.T, beta.T

    row, col = iota((steps, steps), 0), iota((steps, steps), 1)
    eye, strict = row == col, row > col
    levels = []
    size = 1
    while size < steps:
        levels.append(((row // size) % 2 == 1) & ((row // size) - 1 == col // size))
        size *= 2
    token = iota((span, steps), 0)
    visible = 2 * token + 1 >= iota((span, steps), 1)

    blocks = [(h, c) for c in range(chunks) for h in range(heads)]

    def cut(h, c):
        k = k_ref[c * steps : (c + 1) * steps, h * DH : (h + 1) * DH]
        q = q_ref[c * span : (c + 1) * span, h * DH : (h + 1) * DH]
        v = v_ref[c * steps : (c + 1) * steps, h * DH : (h + 1) * DH]
        return q, k, v

    data = {}
    for h, c in blocks:
        q, k, v = cut(h, c)
        inner = lax.dot_general(
            jnp.concatenate([k, q], axis=0), k, (((1,), (1,)), ((), ())), preferred_element_type=F32
        )
        key_inner, query_inner = inner[:steps], inner[steps:]
        diag = jnp.where(eye, key_inner, 0.0)
        scale_row = lax.rsqrt(jnp.sum(diag, axis=0, keepdims=True) + 1e-06)
        scale_col = lax.rsqrt(jnp.sum(diag, axis=1, keepdims=True) + 1e-06)
        cum_row = cum[h : h + 1, c * steps : (c + 1) * steps]
        cum_col = cum_columns[c * steps : (c + 1) * steps, h : h + 1]
        read_col = read_columns[c * span : (c + 1) * span, h : h + 1]
        beta_row = beta[h : h + 1, c * steps : (c + 1) * steps]
        beta_col = beta_columns[c * steps : (c + 1) * steps, h : h + 1]
        weight_row = beta_row * scale_row
        gaps = jnp.exp(jnp.where(strict, cum_col - cum_row, 0.0))
        lower = jnp.where(strict, gaps * key_inner * scale_col * weight_row, 0.0)
        gaps = jnp.exp(jnp.where(visible, read_col - cum_row, 0.0))
        scores = jnp.where(visible, gaps * query_inner * weight_row, 0.0)
        total = cum[h : h + 1, (c + 1) * steps - 1 : (c + 1) * steps]
        into = jnp.exp(total - cum_col) * beta_col * scale_col
        inverse = jnp.where(eye, 1.0, 0.0) - jnp.where(levels[0], lower, 0.0)
        data[h, c] = dict(
            lower=lower, inverse=inverse, scores=scores, into=into, total=jnp.exp(total),
            read=jnp.exp(read_col), carry=jnp.exp(cum_row) * scale_row,
        )
    for level in levels[1:]:
        for b in blocks:
            d = data[b]
            d["part"] = mm_split(jnp.where(level, d["lower"], 0.0), d["inverse"])
        for b in blocks:
            d = data[b]
            d["inverse"] = d["inverse"] - mm_split(d["inverse"], d["part"])
    for h, c in blocks:
        d = data[h, c]
        q, k, v = cut(h, c)
        high, low = halves(d["inverse"])
        d["fresh"] = mm(jnp.concatenate([high, low], axis=1), jnp.concatenate([v, v], axis=0))
        high, low = halves(d["inverse"] * d["carry"])
        d["carried"] = mm(jnp.concatenate([high, low], axis=1), jnp.concatenate([k, k], axis=0))

    zero = jnp.zeros((steps, DH), F32)
    state = [jnp.concatenate([jnp.where(iota((DH, DH), 0) == iota((DH, DH), 1), 1.0, 0.0), jnp.zeros((DH, DH), F32)], axis=1)] * heads
    for c in range(chunks):
        for h in range(heads):
            d = data[h, c]
            q, k, v = cut(h, c)
            s_high, s_low = halves(state[h])
            w_high, w_low = halves(d["carried"])
            moved = mm(
                jnp.concatenate([w_high, w_low], axis=1), jnp.concatenate([s_high, s_high], axis=0)
            ) + mm(w_high, s_low)
            new = jnp.concatenate([zero, d["fresh"]], axis=1) - moved
            seen = d["read"] * (mm(q, s_high) + mm(q, s_low)) + mm(d["scores"].astype(BF16), new.astype(BF16))
            rows = slice(c * span, (c + 1) * span)
            lead_ref[h, rows, :] = seen[:, :DH].astype(BF16)
            loc_ref[h, rows, :] = seen[:, DH:]
            n_high, n_low = halves(new * d["into"])
            turned = k.T
            state[h] = d["total"] * state[h] + mm(
                jnp.concatenate([turned, turned], axis=1), jnp.concatenate([n_high, n_low], axis=0)
            )
    for h in range(heads):
        m_ref[h] = state[h][:, :DH]
        o_ref[h] = state[h][:, DH:]


def local_terms(queries, keys, values, beta, log_gate):
    heads, tokens = log_gate.shape
    shape = jax.ShapeDtypeStruct
    return pl.pallas_call(
        functools.partial(local_kernel, heads, tokens),
        out_shape=(
            shape((heads, tokens, DH), BF16),
            shape((heads, tokens, DH), F32),
            shape((heads, DH, DH), F32),
            shape((heads, DH, DH), F32),
        ),
        in_specs=[pl.BlockSpec(memory_space=pltpu.VMEM)] * 5,
        out_specs=[pl.BlockSpec(memory_space=pltpu.VMEM)] * 4,
        compiler_params=pltpu.CompilerParams(vmem_limit_bytes=40 * 2**20),
        name="local_terms",
    )(queries, keys.reshape(2 * tokens, -1), values.reshape(2 * tokens, -1), beta, log_gate)


def shifted(block, axis, distance):
    devices = range(lax.axis_size(axis))
    route = [(i - distance, i) for i in devices if i - distance in devices]
    return lax.ppermute(block, axis, route)


def on_device(queries, keys, values, beta, log_gate, norm_gain, out_weight):
    heads, tokens = log_gate.shape
    lead, local_part, device_map, device_offset = local_terms(queries, keys, values, beta, log_gate)

    def relay_state(turn_index, incoming):
        leaving = (
            jnp.einsum("hij,hjk->hik", device_map, incoming, precision=highest) + device_offset
        )
        return shifted(leaving.astype(BF16), "ctx", 1).astype(leaving.dtype)

    incoming = lax.fori_loop(
        0, lax.axis_size("ctx") - 1, relay_state, jnp.zeros((heads, DH, DH), F32)
    )
    read_rows = jnp.einsum("htd,hde->hte", lead, incoming.astype(BF16), preferred_element_type=F32) + local_part
    row_scale = lax.rsqrt(jnp.mean(read_rows * read_rows, axis=-1, keepdims=True) + 1e-06)
    normed = (read_rows * row_scale * norm_gain.reshape(heads, 1, DH)).astype(BF16)
    flat_rows = jnp.transpose(normed, (1, 0, 2)).reshape(tokens, heads * DH)
    return lax.psum_scatter(
        jnp.dot(flat_rows, out_weight, preferred_element_type=F32).astype(BF16),
        "head",
        scatter_dimension=0,
        tiled=True,
    )


def solution(mesh):
    return jax.shard_map(
        on_device,
        mesh=mesh,
        in_specs=(
            P("ctx", "head"),
            P("ctx", None, "head"),
            P("ctx", None, "head"),
            P("head", None, "ctx"),
            P("head", "ctx"),
            P("head"),
            P("head", None),
        ),
        out_specs=P(("ctx", "head"), None),
        check_vma=False,
    )
```

```python
import functools

import jax
import jax.numpy as jnp
from jax import lax
from jax.experimental import pallas as pl
from jax.experimental.pallas import tpu as pltpu
from jax.sharding import PartitionSpec as P

DH = 128
F32 = jnp.float32
BF16 = jnp.bfloat16
highest = lax.Precision.HIGHEST


def mm(a, b):
    return jnp.dot(a, b, preferred_element_type=F32)


def halves(x):
    high = x.astype(BF16)
    return high, (x - high.astype(F32)).astype(BF16)


def mm_split(a, b):
    a_high, a_low = halves(a)
    b_high, b_low = halves(b)
    left = jnp.concatenate([a_high, a_low], axis=1)
    row = jnp.concatenate([b_high, b_low], axis=1)
    wide = mm(left, jnp.concatenate([row, row], axis=0))
    n = b.shape[1]
    return wide[:, :n] + wide[:, n:]


def iota(shape, axis):
    return lax.broadcasted_iota(jnp.int32, shape, axis)


def local_kernel(heads, tokens, q_ref, k_ref, v_ref, beta_ref, gate_ref, lead_ref, loc_ref, m_ref, o_ref):
    span = 64 if tokens % 64 == 0 else tokens
    steps = 2 * span
    chunks = tokens // span
    gate = jnp.maximum(gate_ref[...], -1000.0)
    t_at, s_at = iota((tokens, 2 * tokens), 0), iota((tokens, 2 * tokens), 1)
    same = (t_at // span) == (s_at // steps)
    until = (same & (2 * t_at <= s_at)).astype(F32)
    exact = functools.partial(jnp.dot, precision=highest, preferred_element_type=F32)
    cum = exact(gate, until)
    beta = exact(beta_ref[:, 0, :], (2 * t_at == s_at).astype(F32)) + exact(
        beta_ref[:, 1, :], (2 * t_at + 1 == s_at).astype(F32)
    )
    r_at, c_at = iota((tokens, tokens), 0), iota((tokens, tokens), 1)
    read = exact(gate, (((r_at // span) == (c_at // span)) & (r_at <= c_at)).astype(F32))
    pad = jnp.zeros((8 - heads % 8, 2 * tokens), F32) if heads % 8 else None
    if pad is not None:
        cum_columns = jnp.concatenate([cum, pad], axis=0).T
        read_columns = jnp.concatenate([read, pad[:, :tokens]], axis=0).T
        beta_columns = jnp.concatenate([beta, pad], axis=0).T
    else:
        cum_columns, read_columns, beta_columns = cum.T, read.T, beta.T

    row, col = iota((steps, steps), 0), iota((steps, steps), 1)
    eye, strict = row == col, row > col
    levels = []
    size = 1
    while size < steps:
        levels.append(((row // size) % 2 == 1) & ((row // size) - 1 == col // size))
        size *= 2
    token = iota((span, steps), 0)
    visible = 2 * token + 1 >= iota((span, steps), 1)

    blocks = [(h, c) for c in range(chunks) for h in range(heads)]

    def cut(h, c):
        k = k_ref[c * steps : (c + 1) * steps, h * DH : (h + 1) * DH]
        q = q_ref[c * span : (c + 1) * span, h * DH : (h + 1) * DH]
        v = v_ref[c * steps : (c + 1) * steps, h * DH : (h + 1) * DH]
        return q, k, v

    data = {}
    for h, c in blocks:
        q, k, v = cut(h, c)
        inner = lax.dot_general(
            jnp.concatenate([k, q], axis=0), k, (((1,), (1,)), ((), ())), preferred_element_type=F32
        )
        key_inner, query_inner = inner[:steps], inner[steps:]
        diag = jnp.where(eye, key_inner, 0.0)
        scale_row = lax.rsqrt(jnp.sum(diag, axis=0, keepdims=True) + 1e-06)
        scale_col = lax.rsqrt(jnp.sum(diag, axis=1, keepdims=True) + 1e-06)
        cum_row = cum[h : h + 1, c * steps : (c + 1) * steps]
        cum_col = cum_columns[c * steps : (c + 1) * steps, h : h + 1]
        read_col = read_columns[c * span : (c + 1) * span, h : h + 1]
        beta_row = beta[h : h + 1, c * steps : (c + 1) * steps]
        beta_col = beta_columns[c * steps : (c + 1) * steps, h : h + 1]
        weight_row = beta_row * scale_row
        gaps = jnp.exp(jnp.where(strict, cum_col - cum_row, 0.0))
        lower = jnp.where(strict, gaps * key_inner * scale_col * weight_row, 0.0)
        gaps = jnp.exp(jnp.where(visible, read_col - cum_row, 0.0))
        scores = jnp.where(visible, gaps * query_inner * weight_row, 0.0)
        total = cum[h : h + 1, (c + 1) * steps - 1 : (c + 1) * steps]
        into = jnp.exp(total - cum_col) * beta_col * scale_col
        inverse = jnp.where(eye, 1.0, 0.0) - jnp.where(levels[0], lower, 0.0)
        data[h, c] = dict(
            lower=lower, inverse=inverse, scores=scores, into=into, total=jnp.exp(total),
            read=jnp.exp(read_col), carry=jnp.exp(cum_row) * scale_row,
        )
    for level in levels[1:]:
        for b in blocks:
            d = data[b]
            d["part"] = mm_split(jnp.where(level, d["lower"], 0.0), d["inverse"])
        for b in blocks:
            d = data[b]
            d["inverse"] = d["inverse"] - mm_split(d["inverse"], d["part"])
    for h, c in blocks:
        d = data[h, c]
        q, k, v = cut(h, c)
        high, low = halves(d["inverse"])
        d["fresh"] = mm(jnp.concatenate([high, low], axis=1), jnp.concatenate([v, v], axis=0))
        high, low = halves(d["inverse"] * d["carry"])
        d["carried"] = mm(jnp.concatenate([high, low], axis=1), jnp.concatenate([k, k], axis=0))

    zero = jnp.zeros((steps, DH), F32)
    state = [jnp.concatenate([jnp.where(iota((DH, DH), 0) == iota((DH, DH), 1), 1.0, 0.0), jnp.zeros((DH, DH), F32)], axis=1)] * heads
    for c in range(chunks):
        for h in range(heads):
            d = data[h, c]
            q, k, v = cut(h, c)
            s_high, s_low = halves(state[h])
            w_high, w_low = halves(d["carried"])
            moved = mm(
                jnp.concatenate([w_high, w_low], axis=1), jnp.concatenate([s_high, s_high], axis=0)
            ) + mm(w_high, s_low)
            new = jnp.concatenate([zero, d["fresh"]], axis=1) - moved
            seen = d["read"] * (mm(q, s_high) + mm(q, s_low)) + mm(d["scores"].astype(BF16), new.astype(BF16))
            rows = slice(c * span, (c + 1) * span)
            lead_ref[h, rows, :] = seen[:, :DH].astype(BF16)
            loc_ref[h, rows, :] = seen[:, DH:]
            n_high, n_low = halves(new * d["into"])
            turned = k.T
            state[h] = d["total"] * state[h] + mm(
                jnp.concatenate([turned, turned], axis=1), jnp.concatenate([n_high, n_low], axis=0)
            )
    for h in range(heads):
        m_ref[h] = state[h][:, :DH]
        o_ref[h] = state[h][:, DH:]


def local_terms(queries, keys, values, beta, log_gate):
    heads, tokens = log_gate.shape
    shape = jax.ShapeDtypeStruct
    return pl.pallas_call(
        functools.partial(local_kernel, heads, tokens),
        out_shape=(
            shape((heads, tokens, DH), BF16),
            shape((heads, tokens, DH), F32),
            shape((heads, DH, DH), F32),
            shape((heads, DH, DH), F32),
        ),
        in_specs=[pl.BlockSpec(memory_space=pltpu.VMEM)] * 5,
        out_specs=[pl.BlockSpec(memory_space=pltpu.VMEM)] * 4,
        compiler_params=pltpu.CompilerParams(vmem_limit_bytes=40 * 2**20),
        name="local_terms",
    )(queries, keys.reshape(2 * tokens, -1), values.reshape(2 * tokens, -1), beta, log_gate)


def finish_kernel(
    n_ctx, n_head, lead_ref, loc_ref, m_ref, o_ref, gain_ref, w_hbm, out_ref,
    pair_send, pair_recv, joined, state_recv, state_send, normed, weight, part, recv,
    weight_sem, pair_send_sem, pair_recv_sem, state_send_sem, state_recv_sem, row_send_sem, row_recv_sem,
):
    heads = lead_ref.shape[0]
    pieces, _, block, width = part.shape
    me = lax.axis_index("ctx")
    at = lax.axis_index("head")
    odd = lax.rem(me, 2) == 1
    has_prev, has_next = me >= 2, me < n_ctx - 2

    barrier = pltpu.get_barrier_semaphore()
    around = [
        (me >= 1, {"ctx": me - 1}),
        (me < n_ctx - 1, {"ctx": me + 1}),
        (odd & has_prev, {"ctx": me - 2}),
        (odd & has_next, {"ctx": me + 2}),
        (at >= 1, {"head": at - 1}),
        (at < n_head - 1, {"head": at + 1}),
    ]
    count = 0
    for there, device in around:
        count = count + jnp.where(there, 1, 0)

        @pl.when(there)
        def _(device=device):
            pl.semaphore_signal(barrier, inc=1, device_id=device, device_id_type=pl.DeviceIdType.MESH)

    load = pltpu.make_async_copy(w_hbm, weight, weight_sem)
    load.start()
    pl.semaphore_wait(barrier, count)

    def remote(src, dst, send_sem, recv_sem, device):
        return pltpu.make_async_remote_copy(
            src_ref=src, dst_ref=dst, send_sem=send_sem, recv_sem=recv_sem,
            device_id=device, device_id_type=pl.DeviceIdType.MESH,
        )

    def pair_copy(h):
        return remote(pair_send.at[h], pair_recv.at[h], pair_send_sem.at[h], pair_recv_sem.at[h], {"ctx": me + 1})

    def state_copy(h, ahead):
        return remote(
            state_send.at[h], state_recv.at[h], state_send_sem.at[ahead - 1, h], state_recv_sem.at[h], {"ctx": me + ahead}
        )

    @pl.when(jnp.logical_not(odd))
    def _():
        for h in range(heads):
            pair_send[h, :, :DH] = m_ref[h].astype(BF16)
            pair_send[h, :, DH:] = o_ref[h].astype(BF16)
            pair_copy(h).start()

    @pl.when(jnp.logical_not(has_prev))
    def _():
        state_recv[...] = jnp.zeros_like(state_recv)

    @pl.when(odd)
    def _():
        for h in range(heads):
            pair_copy(h).wait_recv()
            high, low = halves(m_ref[h])
            first = pair_recv[h]
            joined[h] = mm(jnp.concatenate([high, low], axis=1), jnp.concatenate([first, first], axis=0))

    @pl.when(odd & has_next)
    def _():
        for h in range(heads):
            high, low = halves(joined[h, :, :DH])
            both = jnp.concatenate([high, low], axis=1)
            offset = joined[h, :, DH:] + o_ref[h]

            @pl.when(has_prev)
            def _():
                state_copy(h, 2).wait_recv()

            state = state_recv[h]
            state_send[h] = (mm(both, jnp.concatenate([state, state], axis=0)) + offset).astype(BF16)
            state_copy(h, 2).start()
            state_copy(h, 1).start()

    @pl.when(has_prev & jnp.logical_not(odd & has_next))
    def _():
        for h in range(heads):
            state_copy(h, 2).wait_recv()

    @pl.when(odd)
    def _():
        for h in range(heads):
            state_recv[h] = (mm(pair_recv[h, :, :DH], state_recv[h]) + pair_recv[h, :, DH:].astype(F32)).astype(BF16)

    for h in range(heads):
        read = mm(lead_ref[h], state_recv[h]) + loc_ref[h]
        scale = lax.rsqrt(jnp.mean(read * read, axis=-1, keepdims=True) + 1e-06)
        columns = slice(h * DH, (h + 1) * DH)
        normed[:, columns] = (read * scale * gain_ref[:, columns]).astype(BF16)
    load.wait()

    def row_copy(p, r, to, slot):
        return remote(part.at[p, r], recv.at[p, slot], row_send_sem.at[p, r], row_recv_sem.at[p, slot], {"head": to})

    def each_row(p, way):
        for r in range(n_head):
            @pl.when(at < r)
            def _(r=r):
                way(row_copy(p, r, at + 1, r))

            @pl.when(at > r)
            def _(r=r):
                way(row_copy(p, r, at - 1, jnp.where(at - 1 == r, n_head, r)))

    def add(p, r, slot):
        row_copy(p, r, at, slot).wait_recv()
        part[p, r] = (part[p, r].astype(F32) + recv[p, slot].astype(F32)).astype(BF16)

    def piece(p, carry):
        @pl.when(p >= 2)
        def _():
            each_row(p - 2, lambda copy: copy.wait_send())

        columns = pl.ds(pl.multiple_of(p * width, width), width)
        rows = mm(normed[...], weight[:, columns]).astype(BF16)
        for r in range(n_head):
            part[p, r] = rows[r * block : (r + 1) * block]
        for j in range(1, n_head):
            right, left = n_head - j, j - 1

            @pl.when(at < right)
            def _():
                @pl.when(at >= 1)
                def _():
                    add(p, right, right)

                row_copy(p, right, at + 1, right).start()

            @pl.when(at > left)
            def _():
                @pl.when(at < n_head - 1)
                def _():
                    add(p, left, left)

                row_copy(p, left, at - 1, jnp.where(at - 1 == left, n_head, left)).start()

        return carry

    lax.fori_loop(0, pieces, piece, 0)

    def last(p, carry):
        columns = pl.ds(pl.multiple_of(p * width, width), width)
        for r in range(n_head):
            @pl.when(at == r)
            def _(r=r):
                total = part[p, r].astype(F32)
                if r >= 1:
                    row_copy(p, r, at, r).wait_recv()
                    total = total + recv[p, r].astype(F32)
                if r < n_head - 1:
                    row_copy(p, r, at, n_head).wait_recv()
                    total = total + recv[p, n_head].astype(F32)
                out_ref[:, columns] = total.astype(BF16)

        return carry

    lax.fori_loop(0, pieces, last, 0)
    for p in range(max(pieces - 2, 0), pieces):
        each_row(p, lambda copy: copy.wait_send())

    @pl.when(jnp.logical_not(odd))
    def _():
        for h in range(heads):
            pair_copy(h).wait_send()

    @pl.when(odd & has_next)
    def _():
        for h in range(heads):
            state_copy(h, 2).wait_send()
            state_copy(h, 1).wait_send()


def finish(n_ctx, n_head, lead, local_part, device_map, device_offset, norm_gain, out_weight):
    heads, tokens, _ = lead.shape
    columns = out_weight.shape[1]
    pieces = 8 if columns % 1024 == 0 else 1
    width, block = columns // pieces, tokens // n_head
    dma = pltpu.SemaphoreType.DMA
    return pl.pallas_call(
        functools.partial(finish_kernel, n_ctx, n_head),
        out_shape=jax.ShapeDtypeStruct((block, columns), BF16),
        in_specs=[pl.BlockSpec(memory_space=pltpu.VMEM)] * 5 + [pl.BlockSpec(memory_space=pl.ANY)],
        out_specs=pl.BlockSpec(memory_space=pltpu.VMEM),
        scratch_shapes=[
            pltpu.VMEM((heads, DH, 2 * DH), BF16),
            pltpu.VMEM((heads, DH, 2 * DH), BF16),
            pltpu.VMEM((heads, DH, 2 * DH), F32),
            pltpu.VMEM((heads, DH, DH), BF16),
            pltpu.VMEM((heads, DH, DH), BF16),
            pltpu.VMEM((tokens, heads * DH), BF16),
            pltpu.VMEM(out_weight.shape, BF16),
            pltpu.VMEM((pieces, n_head, block, width), BF16),
            pltpu.VMEM((pieces, n_head + 1, block, width), BF16),
            dma(()),
            dma((heads,)),
            dma((heads,)),
            dma((2, heads)),
            dma((heads,)),
            dma((pieces, n_head)),
            dma((pieces, n_head + 1)),
        ],
        compiler_params=pltpu.CompilerParams(
            collective_id=0, has_side_effects=True, vmem_limit_bytes=40 * 2**20
        ),
        name="finish",
    )(lead, local_part, device_map, device_offset, norm_gain.reshape(1, -1), out_weight)


def on_device(n_ctx, n_head, queries, keys, values, beta, log_gate, norm_gain, out_weight):
    terms = local_terms(queries, keys, values, beta, log_gate)
    return finish(n_ctx, n_head, *terms, norm_gain, out_weight)


def solution(mesh):
    return jax.shard_map(
        functools.partial(on_device, mesh.shape["ctx"], mesh.shape["head"]),
        mesh=mesh,
        in_specs=(
            P("ctx", "head"),
            P("ctx", None, "head"),
            P("ctx", None, "head"),
            P("head", None, "ctx"),
            P("head", "ctx"),
            P("head"),
            P("head", None),
        ),
        out_specs=P(("ctx", "head"), None),
        check_vma=False,
    )
```

```python
import functools

import jax
import jax.numpy as jnp
from jax import lax
from jax.experimental import pallas as pl
from jax.experimental.pallas import tpu as pltpu
from jax.sharding import PartitionSpec as P

DH = 128
F32 = jnp.float32
BF16 = jnp.bfloat16
highest = lax.Precision.HIGHEST


def mm(a, b):
    return jnp.dot(a, b, preferred_element_type=F32)


def halves(x):
    high = x.astype(BF16)
    return high, (x - high.astype(F32)).astype(BF16)


def mm_split(a, b):
    a_high, a_low = halves(a)
    b_high, b_low = halves(b)
    left = jnp.concatenate([a_high, a_low], axis=1)
    row = jnp.concatenate([b_high, b_low], axis=1)
    wide = mm(left, jnp.concatenate([row, row], axis=0))
    n = b.shape[1]
    return wide[:, :n] + wide[:, n:]


def iota(shape, axis):
    return lax.broadcasted_iota(jnp.int32, shape, axis)


def local_kernel(heads, tokens, q_ref, k_ref, v_ref, beta_ref, gate_ref, lead_ref, loc_ref, m_ref, o_ref):
    span = 64 if tokens % 64 == 0 else tokens
    steps = 2 * span
    chunks = tokens // span
    gate = jnp.maximum(gate_ref[...], -1000.0)
    t_at, s_at = iota((tokens, 2 * tokens), 0), iota((tokens, 2 * tokens), 1)
    same = (t_at // span) == (s_at // steps)
    until = (same & (2 * t_at <= s_at)).astype(F32)
    exact = functools.partial(jnp.dot, precision=highest, preferred_element_type=F32)
    cum = exact(gate, until)
    beta = exact(beta_ref[:, 0, :], (2 * t_at == s_at).astype(F32)) + exact(
        beta_ref[:, 1, :], (2 * t_at + 1 == s_at).astype(F32)
    )
    r_at, c_at = iota((tokens, tokens), 0), iota((tokens, tokens), 1)
    read = exact(gate, (((r_at // span) == (c_at // span)) & (r_at <= c_at)).astype(F32))
    pad = jnp.zeros((8 - heads % 8, 2 * tokens), F32) if heads % 8 else None
    if pad is not None:
        cum_columns = jnp.concatenate([cum, pad], axis=0).T
        read_columns = jnp.concatenate([read, pad[:, :tokens]], axis=0).T
        beta_columns = jnp.concatenate([beta, pad], axis=0).T
    else:
        cum_columns, read_columns, beta_columns = cum.T, read.T, beta.T

    row, col = iota((steps, steps), 0), iota((steps, steps), 1)
    eye, strict = row == col, row > col
    levels = []
    size = 1
    while size < steps:
        levels.append(((row // size) % 2 == 1) & ((row // size) - 1 == col // size))
        size *= 2
    token = iota((span, steps), 0)
    visible = 2 * token + 1 >= iota((span, steps), 1)

    blocks = [(h, c) for c in range(chunks) for h in range(heads)]

    def cut(h, c):
        k = k_ref[c * steps : (c + 1) * steps, h * DH : (h + 1) * DH]
        q = q_ref[c * span : (c + 1) * span, h * DH : (h + 1) * DH]
        v = v_ref[c * steps : (c + 1) * steps, h * DH : (h + 1) * DH]
        return q, k, v

    data = {}
    for h, c in blocks:
        q, k, v = cut(h, c)
        inner = lax.dot_general(
            jnp.concatenate([k, q], axis=0), k, (((1,), (1,)), ((), ())), preferred_element_type=F32
        )
        key_inner, query_inner = inner[:steps], inner[steps:]
        diag = jnp.where(eye, key_inner, 0.0)
        scale_row = lax.rsqrt(jnp.sum(diag, axis=0, keepdims=True) + 1e-06)
        scale_col = lax.rsqrt(jnp.sum(diag, axis=1, keepdims=True) + 1e-06)
        cum_row = cum[h : h + 1, c * steps : (c + 1) * steps]
        cum_col = cum_columns[c * steps : (c + 1) * steps, h : h + 1]
        read_col = read_columns[c * span : (c + 1) * span, h : h + 1]
        beta_row = beta[h : h + 1, c * steps : (c + 1) * steps]
        beta_col = beta_columns[c * steps : (c + 1) * steps, h : h + 1]
        weight_row = beta_row * scale_row
        gaps = jnp.exp(jnp.where(strict, cum_col - cum_row, 0.0))
        lower = jnp.where(strict, gaps * key_inner * scale_col * weight_row, 0.0)
        gaps = jnp.exp(jnp.where(visible, read_col - cum_row, 0.0))
        scores = jnp.where(visible, gaps * query_inner * weight_row, 0.0)
        total = cum[h : h + 1, (c + 1) * steps - 1 : (c + 1) * steps]
        into = jnp.exp(total - cum_col) * beta_col * scale_col
        inverse = jnp.where(eye, 1.0, 0.0) - jnp.where(levels[0], lower, 0.0)
        data[h, c] = dict(
            lower=lower, inverse=inverse, scores=scores, into=into, total=jnp.exp(total),
            read=jnp.exp(read_col), carry=jnp.exp(cum_row) * scale_row,
        )
    for level in levels[1:]:
        for b in blocks:
            d = data[b]
            d["part"] = mm_split(jnp.where(level, d["lower"], 0.0), d["inverse"])
        for b in blocks:
            d = data[b]
            d["inverse"] = d["inverse"] - mm_split(d["inverse"], d["part"])
    for h, c in blocks:
        d = data[h, c]
        q, k, v = cut(h, c)
        high, low = halves(d["inverse"])
        d["fresh"] = mm(jnp.concatenate([high, low], axis=1), jnp.concatenate([v, v], axis=0))
        high, low = halves(d["inverse"] * d["carry"])
        d["carried"] = mm(jnp.concatenate([high, low], axis=1), jnp.concatenate([k, k], axis=0))

    zero = jnp.zeros((steps, DH), F32)
    state = [jnp.concatenate([jnp.where(iota((DH, DH), 0) == iota((DH, DH), 1), 1.0, 0.0), jnp.zeros((DH, DH), F32)], axis=1)] * heads
    for c in range(chunks):
        for h in range(heads):
            d = data[h, c]
            q, k, v = cut(h, c)
            s_high, s_low = halves(state[h])
            w_high, w_low = halves(d["carried"])
            moved = mm(
                jnp.concatenate([w_high, w_low], axis=1), jnp.concatenate([s_high, s_high], axis=0)
            ) + mm(w_high, s_low)
            new = jnp.concatenate([zero, d["fresh"]], axis=1) - moved
            seen = d["read"] * (mm(q, s_high) + mm(q, s_low)) + mm(d["scores"].astype(BF16), new.astype(BF16))
            rows = slice(c * span, (c + 1) * span)
            lead_ref[h, rows, :] = seen[:, :DH].astype(BF16)
            loc_ref[h, rows, :] = seen[:, DH:]
            n_high, n_low = halves(new * d["into"])
            turned = k.T
            state[h] = d["total"] * state[h] + mm(
                jnp.concatenate([turned, turned], axis=1), jnp.concatenate([n_high, n_low], axis=0)
            )
    for h in range(heads):
        m_ref[h] = state[h][:, :DH]
        o_ref[h] = state[h][:, DH:]


def local_terms(queries, keys, values, beta, log_gate):
    heads, tokens = log_gate.shape
    shape = jax.ShapeDtypeStruct
    return pl.pallas_call(
        functools.partial(local_kernel, heads, tokens),
        out_shape=(
            shape((heads, tokens, DH), BF16),
            shape((heads, tokens, DH), F32),
            shape((heads, DH, DH), F32),
            shape((heads, DH, DH), F32),
        ),
        in_specs=[pl.BlockSpec(memory_space=pltpu.VMEM)] * 5,
        out_specs=[pl.BlockSpec(memory_space=pltpu.VMEM)] * 4,
        compiler_params=pltpu.CompilerParams(vmem_limit_bytes=40 * 2**20),
        name="local_terms",
    )(queries, keys.reshape(2 * tokens, -1), values.reshape(2 * tokens, -1), beta, log_gate)


def finish_kernel(
    n_ctx, n_head, lead_ref, loc_ref, m_ref, o_ref, gain_ref, w_hbm, out_ref,
    pair_send, pair_recv, joined, state_recv, state_send, normed, weight, part, recv,
    weight_sem, pair_send_sem, pair_recv_sem, state_send_sem, state_recv_sem, row_send_sem, row_recv_sem,
):
    heads = lead_ref.shape[0]
    pieces, _, block, width = part.shape
    me = lax.axis_index("ctx")
    at = lax.axis_index("head")
    odd = lax.rem(me, 2) == 1
    has_prev, has_next = me >= 2, me < n_ctx - 2

    barrier = pltpu.get_barrier_semaphore()
    around = [
        (me >= 1, {"ctx": me - 1}),
        (me < n_ctx - 1, {"ctx": me + 1}),
        (odd & has_prev, {"ctx": me - 2}),
        (odd & has_next, {"ctx": me + 2}),
        (at >= 1, {"head": at - 1}),
        (at < n_head - 1, {"head": at + 1}),
    ]
    count = 0
    for there, device in around:
        count = count + jnp.where(there, 1, 0)

        @pl.when(there)
        def _(device=device):
            pl.semaphore_signal(barrier, inc=1, device_id=device, device_id_type=pl.DeviceIdType.MESH)

    load = pltpu.make_async_copy(w_hbm, weight, weight_sem)
    load.start()
    pl.semaphore_wait(barrier, count)

    def remote(src, dst, send_sem, recv_sem, device):
        return pltpu.make_async_remote_copy(
            src_ref=src, dst_ref=dst, send_sem=send_sem, recv_sem=recv_sem,
            device_id=device, device_id_type=pl.DeviceIdType.MESH,
        )

    def pair_copy(h):
        return remote(pair_send.at[h], pair_recv.at[h], pair_send_sem.at[h], pair_recv_sem.at[h], {"ctx": me + 1})

    def state_copy(h, ahead):
        return remote(
            state_send.at[h], state_recv.at[h], state_send_sem.at[ahead - 1, h], state_recv_sem.at[h], {"ctx": me + ahead}
        )

    @pl.when(jnp.logical_not(odd))
    def _():
        for h in range(heads):
            pair_send[h, :, :DH] = m_ref[h].astype(BF16)
            pair_send[h, :, DH:] = o_ref[h].astype(BF16)
            pair_copy(h).start()

    @pl.when(jnp.logical_not(has_prev))
    def _():
        state_recv[...] = jnp.zeros_like(state_recv)

    @pl.when(odd)
    def _():
        for h in range(heads):
            pair_copy(h).wait_recv()
            high, low = halves(m_ref[h])
            first = pair_recv[h]
            joined[h] = mm(jnp.concatenate([high, low], axis=1), jnp.concatenate([first, first], axis=0))

    @pl.when(odd & has_next)
    def _():
        for h in range(heads):
            high, low = halves(joined[h, :, :DH])
            both = jnp.concatenate([high, low], axis=1)
            offset = joined[h, :, DH:] + o_ref[h]

            @pl.when(has_prev)
            def _():
                state_copy(h, 2).wait_recv()

            state = state_recv[h]
            state_send[h] = (mm(both, jnp.concatenate([state, state], axis=0)) + offset).astype(BF16)
            state_copy(h, 2).start()
            state_copy(h, 1).start()

    @pl.when(has_prev & jnp.logical_not(odd & has_next))
    def _():
        for h in range(heads):
            state_copy(h, 2).wait_recv()

    @pl.when(odd)
    def _():
        for h in range(heads):
            state_recv[h] = (mm(pair_recv[h, :, :DH], state_recv[h]) + pair_recv[h, :, DH:].astype(F32)).astype(BF16)

    for h in range(heads):
        read = mm(lead_ref[h], state_recv[h]) + loc_ref[h]
        scale = lax.rsqrt(jnp.mean(read * read, axis=-1, keepdims=True) + 1e-06)
        columns = slice(h * DH, (h + 1) * DH)
        normed[:, columns] = (read * scale * gain_ref[:, columns]).astype(BF16)
    load.wait()

    def row_copy(p, r, to, slot):
        return remote(part.at[p, r], recv.at[p, slot], row_send_sem.at[p, r], row_recv_sem.at[p, slot], {"head": to})

    def add(p, r, slot):
        row_copy(p, r, at, slot).wait_recv()
        part[p, r] = (part[p, r].astype(F32) + recv[p, slot].astype(F32)).astype(BF16)

    def sends(p, way, right):
        for r in range(n_head):
            @pl.when(at < r if right else at > r)
            def _(r=r):
                to = at + 1 if right else at - 1
                slot = r if right else jnp.where(to == r, n_head, r)
                way(row_copy(p, r, to, slot))

    def flow(p, right):
        @pl.when((p >= 0) & (p < pieces))
        def _():
            @pl.when(p >= 2)
            def _():
                sends(p - 2, lambda copy: copy.wait_send(), right)

            for r in range(n_head - 1, 0, -1) if right else range(n_head - 1):
                @pl.when(at < r if right else at > r)
                def _(r=r):
                    @pl.when(at >= 1 if right else at < n_head - 1)
                    def _():
                        add(p, r, r)

                    to = at + 1 if right else at - 1
                    row_copy(p, r, to, r if right else jnp.where(to == r, n_head, r)).start()

    def step(i, carry):
        @pl.when(i < pieces)
        def _():
            columns = pl.ds(pl.multiple_of(i * width, width), width)
            rows = mm(normed[...], weight[:, columns]).astype(BF16)
            for r in range(n_head):
                part[i, r] = rows[r * block : (r + 1) * block]

        flow(i - at, True)
        flow(i - (n_head - 1 - at), False)
        p = i - n_head

        @pl.when(p >= 0)
        def _():
            columns = pl.ds(pl.multiple_of(p * width, width), width)
            for r in range(n_head):
                @pl.when(at == r)
                def _(r=r):
                    total = part[p, r].astype(F32)
                    if r >= 1:
                        row_copy(p, r, at, r).wait_recv()
                        total = total + recv[p, r].astype(F32)
                    if r < n_head - 1:
                        row_copy(p, r, at, n_head).wait_recv()
                        total = total + recv[p, n_head].astype(F32)
                    out_ref[:, columns] = total.astype(BF16)

        return carry

    lax.fori_loop(0, pieces + n_head, step, 0)
    for p in range(max(pieces - 2, 0), pieces):
        sends(p, lambda copy: copy.wait_send(), True)
        sends(p, lambda copy: copy.wait_send(), False)

    @pl.when(jnp.logical_not(odd))
    def _():
        for h in range(heads):
            pair_copy(h).wait_send()

    @pl.when(odd & has_next)
    def _():
        for h in range(heads):
            state_copy(h, 2).wait_send()
            state_copy(h, 1).wait_send()


def finish(n_ctx, n_head, lead, local_part, device_map, device_offset, norm_gain, out_weight):
    heads, tokens, _ = lead.shape
    columns = out_weight.shape[1]
    pieces = 8 if columns % 1024 == 0 else 1
    width, block = columns // pieces, tokens // n_head
    dma = pltpu.SemaphoreType.DMA
    return pl.pallas_call(
        functools.partial(finish_kernel, n_ctx, n_head),
        out_shape=jax.ShapeDtypeStruct((block, columns), BF16),
        in_specs=[pl.BlockSpec(memory_space=pltpu.VMEM)] * 5 + [pl.BlockSpec(memory_space=pltpu.HBM)],
        out_specs=pl.BlockSpec(memory_space=pltpu.VMEM),
        scratch_shapes=[
            pltpu.VMEM((heads, DH, 2 * DH), BF16),
            pltpu.VMEM((heads, DH, 2 * DH), BF16),
            pltpu.VMEM((heads, DH, 2 * DH), F32),
            pltpu.VMEM((heads, DH, DH), BF16),
            pltpu.VMEM((heads, DH, DH), BF16),
            pltpu.VMEM((tokens, heads * DH), BF16),
            pltpu.VMEM(out_weight.shape, BF16),
            pltpu.VMEM((pieces, n_head, block, width), BF16),
            pltpu.VMEM((pieces, n_head + 1, block, width), BF16),
            dma(()),
            dma((heads,)),
            dma((heads,)),
            dma((2, heads)),
            dma((heads,)),
            dma((pieces, n_head)),
            dma((pieces, n_head + 1)),
        ],
        compiler_params=pltpu.CompilerParams(
            collective_id=0, has_side_effects=True, vmem_limit_bytes=40 * 2**20
        ),
        name="finish",
    )(lead, local_part, device_map, device_offset, norm_gain.reshape(1, -1), out_weight)


def on_device(n_ctx, n_head, queries, keys, values, beta, log_gate, norm_gain, out_weight):
    terms = local_terms(queries, keys, values, beta, log_gate)
    return finish(n_ctx, n_head, *terms, norm_gain, out_weight)


def solution(mesh):
    return jax.shard_map(
        functools.partial(on_device, mesh.shape["ctx"], mesh.shape["head"]),
        mesh=mesh,
        in_specs=(
            P("ctx", "head"),
            P("ctx", None, "head"),
            P("ctx", None, "head"),
            P("head", None, "ctx"),
            P("head", "ctx"),
            P("head"),
            P("head", None),
        ),
        out_specs=P(("ctx", "head"), None),
        check_vma=False,
    )
```

```python
import functools

import jax
import jax.numpy as jnp
from jax import lax
from jax.experimental import pallas as pl
from jax.experimental.pallas import tpu as pltpu
from jax.sharding import PartitionSpec as P

DH = 128
F32 = jnp.float32
BF16 = jnp.bfloat16
highest = lax.Precision.HIGHEST


def mm(a, b):
    return jnp.dot(a, b, preferred_element_type=F32)


def halves(x):
    high = x.astype(BF16)
    return high, (x - high.astype(F32)).astype(BF16)


def mm_split(a, b):
    a_high, a_low = halves(a)
    b_high, b_low = halves(b)
    left = jnp.concatenate([a_high, a_low], axis=1)
    row = jnp.concatenate([b_high, b_low], axis=1)
    wide = mm(left, jnp.concatenate([row, row], axis=0))
    n = b.shape[1]
    return wide[:, :n] + wide[:, n:]


def iota(shape, axis):
    return lax.broadcasted_iota(jnp.int32, shape, axis)


def local_kernel(heads, tokens, q_ref, k_ref, v_ref, beta_ref, gate_ref, lead_ref, loc_ref, m_ref, o_ref):
    span = 64 if tokens % 64 == 0 else tokens
    steps = 2 * span
    chunks = tokens // span
    gate = jnp.maximum(gate_ref[...], -1000.0)
    t_at, s_at = iota((tokens, 2 * tokens), 0), iota((tokens, 2 * tokens), 1)
    same = (t_at // span) == (s_at // steps)
    until = (same & (2 * t_at <= s_at)).astype(F32)
    exact = functools.partial(jnp.dot, precision=highest, preferred_element_type=F32)
    cum = exact(gate, until)
    beta = exact(beta_ref[:, 0, :], (2 * t_at == s_at).astype(F32)) + exact(
        beta_ref[:, 1, :], (2 * t_at + 1 == s_at).astype(F32)
    )
    r_at, c_at = iota((tokens, tokens), 0), iota((tokens, tokens), 1)
    read = exact(gate, (((r_at // span) == (c_at // span)) & (r_at <= c_at)).astype(F32))
    pad = jnp.zeros((8 - heads % 8, 2 * tokens), F32) if heads % 8 else None
    if pad is not None:
        cum_columns = jnp.concatenate([cum, pad], axis=0).T
        read_columns = jnp.concatenate([read, pad[:, :tokens]], axis=0).T
        beta_columns = jnp.concatenate([beta, pad], axis=0).T
    else:
        cum_columns, read_columns, beta_columns = cum.T, read.T, beta.T

    row, col = iota((steps, steps), 0), iota((steps, steps), 1)
    eye, strict = row == col, row > col
    levels = []
    size = 1
    while size < steps:
        levels.append(((row // size) % 2 == 1) & ((row // size) - 1 == col // size))
        size *= 2
    token = iota((span, steps), 0)
    visible = 2 * token + 1 >= iota((span, steps), 1)

    blocks = [(h, c) for c in range(chunks) for h in range(heads)]

    def cut(h, c):
        k = k_ref[c * span : (c + 1) * span, :, h * DH : (h + 1) * DH].reshape(steps, DH)
        q = q_ref[c * span : (c + 1) * span, h * DH : (h + 1) * DH]
        v = v_ref[c * span : (c + 1) * span, :, h * DH : (h + 1) * DH].reshape(steps, DH)
        return q, k, v

    data = {}
    cuts = {b: cut(*b) for b in blocks}
    for h, c in blocks:
        q, k, v = cuts[h, c]
        inner = lax.dot_general(
            jnp.concatenate([k, q], axis=0), k, (((1,), (1,)), ((), ())), preferred_element_type=F32
        )
        key_inner, query_inner = inner[:steps], inner[steps:]
        diag = jnp.where(eye, key_inner, 0.0)
        scale_row = lax.rsqrt(jnp.sum(diag, axis=0, keepdims=True) + 1e-06)
        scale_col = lax.rsqrt(jnp.sum(diag, axis=1, keepdims=True) + 1e-06)
        cum_row = cum[h : h + 1, c * steps : (c + 1) * steps]
        cum_col = cum_columns[c * steps : (c + 1) * steps, h : h + 1]
        read_col = read_columns[c * span : (c + 1) * span, h : h + 1]
        beta_row = beta[h : h + 1, c * steps : (c + 1) * steps]
        beta_col = beta_columns[c * steps : (c + 1) * steps, h : h + 1]
        weight_row = beta_row * scale_row
        gaps = jnp.exp(jnp.where(strict, cum_col - cum_row, 0.0))
        lower = jnp.where(strict, gaps * key_inner * scale_col * weight_row, 0.0)
        gaps = jnp.exp(jnp.where(visible, read_col - cum_row, 0.0))
        scores = jnp.where(visible, gaps * query_inner * weight_row, 0.0)
        total = cum[h : h + 1, (c + 1) * steps - 1 : (c + 1) * steps]
        into = jnp.exp(total - cum_col) * beta_col * scale_col
        inverse = jnp.where(eye, 1.0, 0.0) - jnp.where(levels[0], lower, 0.0)
        data[h, c] = dict(
            lower=lower, inverse=inverse, scores=scores, into=into, total=jnp.exp(total),
            read=jnp.exp(read_col), carry=jnp.exp(cum_row) * scale_row,
        )
    for level in levels[1:]:
        for b in blocks:
            d = data[b]
            d["part"] = mm_split(jnp.where(level, d["lower"], 0.0), d["inverse"])
        for b in blocks:
            d = data[b]
            d["inverse"] = d["inverse"] - mm_split(d["inverse"], d["part"])
    for h, c in blocks:
        d = data[h, c]
        q, k, v = cuts[h, c]
        high, low = halves(d["inverse"])
        d["fresh"] = mm(jnp.concatenate([high, low], axis=1), jnp.concatenate([v, v], axis=0))
        high, low = halves(d["inverse"] * d["carry"])
        d["carried"] = mm(jnp.concatenate([high, low], axis=1), jnp.concatenate([k, k], axis=0))

    zero = jnp.zeros((steps, DH), F32)
    state = [jnp.concatenate([jnp.where(iota((DH, DH), 0) == iota((DH, DH), 1), 1.0, 0.0), jnp.zeros((DH, DH), F32)], axis=1)] * heads
    for c in range(chunks):
        for h in range(heads):
            d = data[h, c]
            q, k, v = cuts[h, c]
            s_high, s_low = halves(state[h])
            w_high, w_low = halves(d["carried"])
            moved = mm(
                jnp.concatenate([w_high, w_low], axis=1), jnp.concatenate([s_high, s_high], axis=0)
            ) + mm(w_high, s_low)
            new = jnp.concatenate([zero, d["fresh"]], axis=1) - moved
            seen = d["read"] * (mm(q, s_high) + mm(q, s_low)) + mm(d["scores"].astype(BF16), new.astype(BF16))
            rows = slice(c * span, (c + 1) * span)
            lead_ref[h, rows, :] = seen[:, :DH].astype(BF16)
            loc_ref[h, rows, :] = seen[:, DH:]
            n_high, n_low = halves(new * d["into"])
            turned = k.T
            state[h] = d["total"] * state[h] + mm(
                jnp.concatenate([turned, turned], axis=1), jnp.concatenate([n_high, n_low], axis=0)
            )
    for h in range(heads):
        m_ref[h] = state[h][:, :DH]
        o_ref[h] = state[h][:, DH:]


def local_terms(queries, keys, values, beta, log_gate):
    heads, tokens = log_gate.shape
    shape = jax.ShapeDtypeStruct
    return pl.pallas_call(
        functools.partial(local_kernel, heads, tokens),
        out_shape=(
            shape((heads, tokens, DH), BF16),
            shape((heads, tokens, DH), F32),
            shape((heads, DH, DH), F32),
            shape((heads, DH, DH), F32),
        ),
        out_specs=[pl.BlockSpec(memory_space=pltpu.VMEM)] * 4,
        compiler_params=pltpu.CompilerParams(vmem_limit_bytes=62 * 2**20),
        name="local_terms",
    )(queries, keys, values, beta, log_gate)


def finish_kernel(
    n_ctx, n_head, lead_ref, loc_ref, m_ref, o_ref, gain_ref, w_hbm, out_ref,
    pair_send, pair_recv, joined, offset, state_recv, state_send, normed, weight, part, recv,
    weight_sem, pair_send_sem, pair_recv_sem, state_send_sem, state_recv_sem, row_send_sem, row_recv_sem,
):
    heads = lead_ref.shape[0]
    pieces, _, block, width = part.shape
    me = lax.axis_index("ctx")
    at = lax.axis_index("head")
    odd = lax.rem(me, 2) == 1
    has_prev, has_next = me >= 2, me < n_ctx - 2

    barrier = pltpu.get_barrier_semaphore()
    around = [
        (me >= 1, {"ctx": me - 1}),
        (me < n_ctx - 1, {"ctx": me + 1}),
        (odd & has_prev, {"ctx": me - 2}),
        (odd & has_next, {"ctx": me + 2}),
        (at >= 1, {"head": at - 1}),
        (at < n_head - 1, {"head": at + 1}),
    ]
    count = 0
    for there, device in around:
        count = count + jnp.where(there, 1, 0)

        @pl.when(there)
        def _(device=device):
            pl.semaphore_signal(barrier, inc=1, device_id=device, device_id_type=pl.DeviceIdType.MESH)

    load = pltpu.make_async_copy(w_hbm, weight, weight_sem)
    load.start()
    pl.semaphore_wait(barrier, count)

    def remote(src, dst, send_sem, recv_sem, device):
        return pltpu.make_async_remote_copy(
            src_ref=src, dst_ref=dst, send_sem=send_sem, recv_sem=recv_sem,
            device_id=device, device_id_type=pl.DeviceIdType.MESH,
        )

    def pair_copy(h):
        return remote(pair_send.at[h], pair_recv.at[h], pair_send_sem.at[h], pair_recv_sem.at[h], {"ctx": me + 1})

    def state_copy(h, ahead):
        return remote(
            state_send.at[h], state_recv.at[h], state_send_sem.at[ahead - 1, h], state_recv_sem.at[h], {"ctx": me + ahead}
        )

    @pl.when(jnp.logical_not(odd))
    def _():
        for h in range(heads):
            pair_send[h, :, :DH] = m_ref[h].astype(BF16)
            pair_send[h, :, DH:] = o_ref[h].astype(BF16)
            pair_copy(h).start()

    @pl.when(jnp.logical_not(has_prev))
    def _():
        state_recv[...] = jnp.zeros_like(state_recv)

    @pl.when(odd)
    def _():
        for h in range(heads):
            pair_copy(h).wait_recv()

    def send_state(h):
        state_copy(h, 2).start()
        state_copy(h, 1).start()

    @pl.when(odd & has_next & jnp.logical_not(has_prev))
    def _():
        for h in range(heads):
            first = pair_recv[h, :, DH:]
            both = jnp.concatenate(halves(m_ref[h]), axis=1)
            state_send[h] = (mm(both, jnp.concatenate([first, first], axis=0)) + o_ref[h]).astype(BF16)
        for h in range(heads):
            send_state(h)

    @pl.when(odd & has_next & has_prev)
    def _():
        for h in range(heads):
            both = jnp.concatenate(halves(m_ref[h]), axis=1)
            first = pair_recv[h]
            wide = mm(both, jnp.concatenate([first, first], axis=0))
            joined[h] = jnp.concatenate(halves(wide[:, :DH]), axis=1)
            offset[h] = wide[:, DH:] + o_ref[h]
        for h in range(heads):
            state_copy(h, 2).wait_recv()
            state = state_recv[h]
            state_send[h] = (mm(joined[h], jnp.concatenate([state, state], axis=0)) + offset[h]).astype(BF16)
            send_state(h)

    @pl.when(has_prev & jnp.logical_not(odd & has_next))
    def _():
        for h in range(heads):
            state_copy(h, 2).wait_recv()

    @pl.when(odd)
    def _():
        for h in range(heads):
            state_recv[h] = (mm(pair_recv[h, :, :DH], state_recv[h]) + pair_recv[h, :, DH:].astype(F32)).astype(BF16)

    for h in range(heads):
        read = mm(lead_ref[h], state_recv[h]) + loc_ref[h]
        scale = lax.rsqrt(jnp.mean(read * read, axis=-1, keepdims=True) + 1e-06)
        columns = slice(h * DH, (h + 1) * DH)
        normed[:, columns] = (read * scale * gain_ref[:, columns]).astype(BF16)
    load.wait()

    def row_copy(p, r, to, slot):
        return remote(part.at[p, r], recv.at[p, slot], row_send_sem.at[p, r], row_recv_sem.at[p, slot], {"head": to})

    def add(p, r, slot):
        row_copy(p, r, at, slot).wait_recv()
        part[p, r] = (part[p, r].astype(F32) + recv[p, slot].astype(F32)).astype(BF16)

    def sends(p, way, right):
        for r in range(n_head):
            @pl.when(at < r if right else at > r)
            def _(r=r):
                to = at + 1 if right else at - 1
                slot = r if right else jnp.where(to == r, n_head, r)
                way(row_copy(p, r, to, slot))

    def flow(p, right):
        @pl.when((p >= 0) & (p < pieces))
        def _():
            @pl.when(p >= 2)
            def _():
                sends(p - 2, lambda copy: copy.wait_send(), right)

            for r in range(n_head - 1, 0, -1) if right else range(n_head - 1):
                @pl.when(at < r if right else at > r)
                def _(r=r):
                    @pl.when(at >= 1 if right else at < n_head - 1)
                    def _():
                        add(p, r, r)

                    to = at + 1 if right else at - 1
                    row_copy(p, r, to, r if right else jnp.where(to == r, n_head, r)).start()

    def step(i, carry):
        @pl.when(i < pieces)
        def _():
            columns = pl.ds(pl.multiple_of(i * width, width), width)
            rows = mm(normed[...], weight[:, columns]).astype(BF16)
            for r in range(n_head):
                part[i, r] = rows[r * block : (r + 1) * block]

        flow(i - at, True)
        flow(i - (n_head - 1 - at), False)
        p = i - n_head

        @pl.when(p >= 0)
        def _():
            columns = pl.ds(pl.multiple_of(p * width, width), width)
            for r in range(n_head):
                @pl.when(at == r)
                def _(r=r):
                    total = part[p, r].astype(F32)
                    if r >= 1:
                        row_copy(p, r, at, r).wait_recv()
                        total = total + recv[p, r].astype(F32)
                    if r < n_head - 1:
                        row_copy(p, r, at, n_head).wait_recv()
                        total = total + recv[p, n_head].astype(F32)
                    out_ref[:, columns] = total.astype(BF16)

        return carry

    lax.fori_loop(0, pieces + n_head, step, 0)
    for p in range(max(pieces - 2, 0), pieces):
        sends(p, lambda copy: copy.wait_send(), True)
        sends(p, lambda copy: copy.wait_send(), False)

    @pl.when(jnp.logical_not(odd))
    def _():
        for h in range(heads):
            pair_copy(h).wait_send()

    @pl.when(odd & has_next)
    def _():
        for h in range(heads):
            state_copy(h, 2).wait_send()
            state_copy(h, 1).wait_send()


def finish(n_ctx, n_head, lead, local_part, device_map, device_offset, norm_gain, out_weight):
    heads, tokens, _ = lead.shape
    columns = out_weight.shape[1]
    pieces = 8 if columns % 1024 == 0 else 1
    width, block = columns // pieces, tokens // n_head
    dma = pltpu.SemaphoreType.DMA
    return pl.pallas_call(
        functools.partial(finish_kernel, n_ctx, n_head),
        out_shape=jax.ShapeDtypeStruct((block, columns), BF16),
        in_specs=[pl.BlockSpec(memory_space=pltpu.VMEM)] * 5 + [pl.BlockSpec(memory_space=pltpu.HBM)],
        out_specs=pl.BlockSpec(memory_space=pltpu.VMEM),
        scratch_shapes=[
            pltpu.VMEM((heads, DH, 2 * DH), BF16),
            pltpu.VMEM((heads, DH, 2 * DH), BF16),
            pltpu.VMEM((heads, DH, 2 * DH), BF16),
            pltpu.VMEM((heads, DH, DH), F32),
            pltpu.VMEM((heads, DH, DH), BF16),
            pltpu.VMEM((heads, DH, DH), BF16),
            pltpu.VMEM((tokens, heads * DH), BF16),
            pltpu.VMEM(out_weight.shape, BF16),
            pltpu.VMEM((pieces, n_head, block, width), BF16),
            pltpu.VMEM((pieces, n_head + 1, block, width), BF16),
            dma(()),
            dma((heads,)),
            dma((heads,)),
            dma((2, heads)),
            dma((heads,)),
            dma((pieces, n_head)),
            dma((pieces, n_head + 1)),
        ],
        compiler_params=pltpu.CompilerParams(
            collective_id=0, has_side_effects=True, vmem_limit_bytes=60 * 2**20
        ),
        name="finish",
    )(lead, local_part, device_map, device_offset, norm_gain.reshape(1, -1), out_weight)


def on_device(n_ctx, n_head, queries, keys, values, beta, log_gate, norm_gain, out_weight):
    terms = local_terms(queries, keys, values, beta, log_gate)
    return finish(n_ctx, n_head, *terms, norm_gain, out_weight)


def solution(mesh):
    return jax.shard_map(
        functools.partial(on_device, mesh.shape["ctx"], mesh.shape["head"]),
        mesh=mesh,
        in_specs=(
            P("ctx", "head"),
            P("ctx", None, "head"),
            P("ctx", None, "head"),
            P("head", None, "ctx"),
            P("head", "ctx"),
            P("head"),
            P("head", None),
        ),
        out_specs=P(("ctx", "head"), None),
        check_vma=False,
    )
```
